256 devices in a mesh: head: 4 (over z_hi, core), inner: 16 (over x, y), outer: 4 (over z_lo).
Axes of the slice: x: 4, y: 4, z: 8 (z_hi: 2, z_lo: 4; z = z_hi * 4 + z_lo), core: 2. Of those that a mesh axis runs over, the one named last changes fastest.
Arguments:
- query: bfloat16 [32768, 3584], P(('head', 'inner', 'outer')), may hold values from -24 to 24
- key: bfloat16 [32768, 512], P(('head', 'inner', 'outer')), may hold values from -9 to 9
- value: bfloat16 [32768, 512], P(('head', 'inner', 'outer')), may hold values from -6 to 6
- vertical_blocks: int32 [4, 8], replicated, may hold values from 0 to 511, as said below
- slash_offsets: int32 [4, 9], replicated, may hold values from 0 to 8, as said below
- block_counts: int32 [4, 2], replicated, may hold values from 1 to 9, as said below
Outputs:
- attended: bfloat16 [32768, 3584], P(('head', 'inner', 'outer'))
The draws below stay inside these ranges and needn't reach their ends.
Inputs may be any that keep to these rules, and one draw needn't show every extreme that they name: `vertical_blocks`: within a row the entries are distinct indices of 64-token blocks; only the first block_counts[h, 0] of row h are used. `slash_offsets`: within a row the entries are distinct and the first is 0; only the first block_counts[h, 1] of row h are used. `block_counts`: column 0 is at most 8, column 1 at most 9.
All inputs are finite; a program needn't handle non-finite values.
Results may differ from the reference program's by a relative error of at most 0.0044.
Values may be sent and summed in bfloat16 or wider, within the bound.
No kernel may reach another device: no remote copies, remote signals or barrier semaphores. Data moves between devices by JAX's collectives and lax.ppermute only.
A program may use at most 64 MiB of HBM per device.

```python
from functools import partial
import jax
import jax.numpy as jnp
from jax import lax

QH = 28
KVH = 4
HD = 128
BLOCK = 64
MAXV = 8
SLASH_REACH = 8
QGROUP = 2
MAXS = 9
SEQ = 32768


def draw_key(key, part):
    key = jax.random.fold_in(key, 3)
    drawn = jax.random.truncated_normal(key, -4.0, 4.0, (SEQ, KVH * HD), jnp.float32)
    return drawn.astype(jnp.bfloat16)


def draw_query(key, part):
    key = jax.random.fold_in(key, 5)
    drawn = jax.random.truncated_normal(key, -4.0, 4.0, (SEQ, QH * HD), jnp.float32)
    return drawn.astype(jnp.bfloat16)


def draw_vertical_blocks(key, part):
    key = jax.random.fold_in(key, 21)
    blocks = SEQ // BLOCK
    keys = jax.random.split(key, KVH + 1)
    table = jnp.stack([jax.random.permutation(keys[head_index], blocks)[:MAXV].astype(jnp.int32) for head_index in range(KVH)])
    picks = jax.random.randint(keys[KVH], (2,), 0, KVH)
    low_head = picks[0]
    high_head = (picks[0] + 1 + picks[1] % (KVH - 1)) % KVH
    heads_column = jnp.arange(KVH, dtype=jnp.int32)[:, None]
    table = jnp.where(heads_column == low_head, (table - table[:, :1]) % blocks, table)
    table = jnp.where(heads_column == high_head, (table - table[:, :1] - 1) % blocks, table)
    return table.astype(jnp.int32)


def draw_slash_offsets(key, part):
    key = jax.random.fold_in(key, 7)
    keys = jax.random.split(key, KVH)
    table = [jnp.concatenate([jnp.zeros((1,), jnp.int32), jax.random.permutation(keys[head_index], SLASH_REACH).astype(jnp.int32) + 1]) for head_index in range(KVH)]
    return jnp.stack(table).astype(jnp.int32)


def draw_block_counts(key, part):
    key = jax.random.fold_in(key, 9)
    first_key, second_key, third_key = jax.random.split(key, 3)
    vertical_count = jax.random.randint(first_key, (KVH,), 1, MAXV + 1)
    slash_count = jax.random.randint(second_key, (KVH,), 1, MAXS + 1)
    picks = jax.random.randint(third_key, (2,), 0, KVH)
    heads_index = jnp.arange(KVH, dtype=jnp.int32)
    vertical_count = jnp.where(heads_index == picks[0], MAXV, vertical_count)
    slash_count = jnp.where(heads_index == picks[1], MAXS, slash_count)
    vertical_count = jnp.where(heads_index == (picks[1] + 1) % KVH, 1, vertical_count)
    return jnp.stack([vertical_count, slash_count], axis=1).astype(jnp.int32)


def shard_levels(stream_key, dims, cuts, smallest, largest):
    gain, own = 1.0, jax.random.fold_in(stream_key, 6)
    for axis_at, shards_of in cuts:
        heights = jnp.exp(jax.random.uniform(jax.random.fold_in(own, axis_at), (shards_of,), jnp.float32, smallest / len(cuts), largest / len(cuts)))
        gain = gain * jnp.repeat(heights, dims[axis_at] // shards_of).reshape([-1 if axis == axis_at else 1 for axis in range(len(dims))])
    return gain


def bell_draw(own_key, dims, width, limit, shards=(), kind=jnp.bfloat16):
    entries = jax.random.normal(own_key, dims, jnp.float32) * width
    if len(shards) > 0:
        entries = shard_levels(own_key, dims, shards, -0.22, 0.18) * entries
    return jnp.clip(entries, min=-limit, max=limit).astype(kind)


def setup_inputs(seed: int = 0) -> dict:
    streams_of = jax.random.split(jax.random.key(seed), 7)
    return {
        "query": draw_query(jax.random.fold_in(streams_of[6], 71), 0),
        "key": draw_key(jax.random.fold_in(streams_of[6], 71), 0),
        "value": bell_draw(streams_of[2], (SEQ, KVH * HD), 1.0, 6.0, ((0, 256),)),
        "vertical_blocks": draw_vertical_blocks(jax.random.fold_in(streams_of[6], 71), 0),
        "slash_offsets": draw_slash_offsets(jax.random.fold_in(streams_of[6], 71), 0),
        "block_counts": draw_block_counts(jax.random.fold_in(streams_of[6], 71), 0),
    }


NEGATIVE = -1e30


def head_group(query_blocks, key_blocks, value_blocks, vertical, offsets, vertical_count, slash_count, group):
    first_block = group * QGROUP
    queries = lax.dynamic_slice_in_dim(query_blocks, first_block, QGROUP, 0)
    query_ids = first_block + jnp.arange(QGROUP, dtype=jnp.int32)
    vertical_live = (jnp.arange(MAXV, dtype=jnp.int32) < vertical_count)[None, :] & (vertical[None, :] <= query_ids[:, None])
    slash_ids = query_ids[:, None] - offsets[None, :]
    doubled = jnp.any((slash_ids[:, :, None] == vertical[None, None, :]) & vertical_live[:, None, :], axis=2)
    slash_live = (jnp.arange(MAXS, dtype=jnp.int32) < slash_count)[None, :] & (slash_ids >= 0) & jnp.logical_not(doubled)
    safe_ids = jnp.maximum(slash_ids, 0)
    chosen = jnp.concatenate([jnp.broadcast_to(vertical[None, :], (QGROUP, MAXV)), safe_ids], axis=1)
    live_blocks = jnp.concatenate([vertical_live, slash_live], axis=1)
    picked_keys = key_blocks[chosen].reshape(QGROUP, (MAXV + MAXS) * BLOCK, HD)
    picked_values = value_blocks[chosen].reshape(QGROUP, (MAXV + MAXS) * BLOCK, HD)
    within = jnp.arange(BLOCK, dtype=jnp.int32)
    key_pos = (chosen[:, :, None] * BLOCK + within[None, None, :]).reshape(QGROUP, (MAXV + MAXS) * BLOCK)
    key_live = jnp.repeat(live_blocks, BLOCK, axis=1)
    query_pos = query_ids[:, None] * BLOCK + within[None, :]
    allowed = (key_live[:, None, :] & (key_pos[:, None, :] <= query_pos[:, :, None]))[:, :, None, :]
    scores = jnp.einsum("qbrd,qnd->qbrn", queries.astype(jnp.float32), picked_keys.astype(jnp.float32)) * (HD ** -0.5)
    highest = jnp.max(jnp.where(allowed, scores, NEGATIVE), axis=-1, keepdims=True)
    weights = jnp.where(allowed, jnp.exp(scores - highest), 0.0)
    totals = jnp.sum(weights, axis=-1)
    rounded = lax.optimization_barrier(weights.astype(jnp.bfloat16))
    attended = jnp.einsum("qbrn,qnd->qbrd", rounded.astype(jnp.float32), picked_values.astype(jnp.float32)) / totals[..., None]
    return attended.astype(jnp.bfloat16)


def reference(query, key, value, vertical_blocks, slash_offsets, block_counts):
    blocks = SEQ // BLOCK
    per_group = QH // KVH
    pieces = []
    for head_index in range(KVH):
        query_blocks = query[:, head_index * per_group * HD:(head_index + 1) * per_group * HD].reshape(blocks, BLOCK, per_group, HD)
        key_blocks = key[:, head_index * HD:(head_index + 1) * HD].reshape(blocks, BLOCK, HD)
        value_blocks = value[:, head_index * HD:(head_index + 1) * HD].reshape(blocks, BLOCK, HD)
        group_step = partial(head_group, query_blocks, key_blocks, value_blocks, vertical_blocks[head_index], slash_offsets[head_index], block_counts[head_index, 0], block_counts[head_index, 1])
        attended = lax.map(group_step, jnp.arange(blocks // QGROUP, dtype=jnp.int32))
        pieces.append(attended.reshape(SEQ, per_group * HD))
    return jnp.concatenate(pieces, axis=1)
```

```python
import math
import jax
import jax.numpy as jnp
import numpy as np
from jax import lax
from jax.experimental import pallas as pl
from jax.experimental.pallas import tpu as pltpu
from jax.sharding import Mesh, PartitionSpec as P

QH = 28
KVH = 4
HD = 128
BLOCK = 64
MAXV = 8
MAXS = 9
PER = QH // KVH
SIZES = (2, 2, 4, 4, 4)
AXES = ("zh", "c", "x", "y", "zl")
DEVICES = 256
CHUNK = 4
CAPACITY = 5 * CHUNK
NEGATIVE = -1e30
LOG2_SCALE = math.log2(math.e) * HD ** (-0.5)
VMEM = pl.BlockSpec(memory_space=pltpu.VMEM)
SMEM = pl.BlockSpec(memory_space=pltpu.SMEM)
ANY = pl.BlockSpec(memory_space=pl.ANY)


def owner_plane(block):
    return (block >> 3) & 31


def owner_layer(block):
    return ((block >> 8) << 2) | ((block >> 1) & 3)


def pack_kernel(key_ref, value_ref, packed_ref):
    for h in range(KVH):
        for kv, source in enumerate((key_ref, value_ref)):
            for quarter in range(4):
                for block in range(2):
                    packed_ref[h * 8 + kv * 4 + quarter, block * 16 : block * 16 + 16, :] = source[
                        block * 64 + quarter * 16 : block * 64 + quarter * 16 + 16,
                        h * HD : (h + 1) * HD,
                    ]


def pick_owned_kernel(place_ref, vertical_ref, received_ref, out_ref):
    head = place_ref[0] >> 3
    for j in range(MAXV):
        block = vertical_ref[head, j]
        piece = received_ref[owner_plane(block), block & 1]
        for copy in range(8):
            out_ref[copy, j] = piece


def pick_layer_kernel(place_ref, vertical_ref, received_ref, out_ref):
    head = place_ref[0] >> 3
    for j in range(MAXV):
        piece = received_ref[owner_layer(vertical_ref[head, j]), j]
        for copy in range(16):
            out_ref[copy, j] = piece


def attend_kernel(
    place_ref,
    vertical_ref,
    offsets_ref,
    counts_ref,
    query_ref,
    own_ref,
    second_ref,
    fourth_ref,
    odd_ref,
    near_ref,
    far_ref,
    out_ref,
    slab,
    pairs,
    keys,
    values,
    sems,
):
    step = pl.program_id(0)
    device = place_ref[1]
    half = step >> 1
    low = step & 1
    head = (((place_ref[0] >> 4) ^ half) << 1) | low

    @pl.when(step == 0)
    def _():
        copies = [
            pltpu.make_async_copy(fourth_ref, slab.at[0], sems.at[0]),
            pltpu.make_async_copy(odd_ref.at[1], slab.at[1], sems.at[1]),
            pltpu.make_async_copy(second_ref, slab.at[2], sems.at[2]),
            pltpu.make_async_copy(odd_ref.at[0], slab.at[3], sems.at[3]),
            pltpu.make_async_copy(own_ref, slab.at[4], sems.at[4]),
            pltpu.make_async_copy(near_ref, pairs.at[0], sems.at[5]),
            pltpu.make_async_copy(far_ref, pairs.at[1], sems.at[6]),
        ]
        for copy in copies:
            copy.start()
        keys[...] = jnp.zeros_like(keys)
        values[:, :HD] = jnp.zeros((CAPACITY * BLOCK, HD), jnp.bfloat16)
        values[:, HD:] = jnp.ones((CAPACITY * BLOCK, HD), jnp.bfloat16)
        for copy in copies:
            copy.wait()

    def put(slot, key, value):
        rows = pl.ds(pl.multiple_of(slot * BLOCK, BLOCK), BLOCK)
        keys[rows, :] = key.reshape(BLOCK, HD)
        values[rows, :HD] = value.reshape(BLOCK, HD)

    for local_block in range(2):
        block = device * 2 + local_block
        put(0, slab[4, head, 0, :, local_block], slab[4, head, 1, :, local_block])
        filled = jnp.int32(1)
        near = jnp.int32(0)
        for j in range(MAXV):
            vertical = vertical_ref[head, j]
            put(filled, pairs[half, low, 0, :, j], pairs[half, low, 1, :, j])
            live = (j < counts_ref[head, 0]) & (vertical < block)
            distance = block - vertical
            near = jnp.where(live & (distance <= 8), near | (1 << jnp.clip(distance, 0, 8)), near)
            filled = jnp.where(live, filled + 1, filled)
        for i in range(1, MAXS):
            offset = offsets_ref[head, i]
            live = (
                (i < counts_ref[head, 1]) & (block >= offset) & (((near >> offset) & 1) == 0)
            )
            place = local_block + 8 - offset
            put(
                filled,
                slab[place >> 1, head, 0, :, place & 1],
                slab[place >> 1, head, 1, :, place & 1],
            )
            filled = jnp.where(live, filled + 1, filled)

        rows = slice(local_block * BLOCK, (local_block + 1) * BLOCK)
        queries = jnp.concatenate(
            [query_ref[rows, r * HD : (r + 1) * HD] for r in range(PER)], axis=0
        )

        def run(chunks):
            width = CHUNK * BLOCK
            total = PER * BLOCK
            scores = []
            for chunk in range(chunks):
                part = lax.dot_general(
                    queries,
                    keys[chunk * width : (chunk + 1) * width, :],
                    (((1,), (1,)), ((), ())),
                    preferred_element_type=jnp.float32,
                )
                if chunk == 0 or chunk == chunks - 1:
                    lane = lax.broadcasted_iota(jnp.int32, (total, width), 1)
                    allowed = lane + chunk * width < filled * BLOCK
                    if chunk == 0:
                        token = lax.broadcasted_iota(jnp.int32, (total, width), 0) % BLOCK
                        allowed = allowed & ((lane >= BLOCK) | (lane <= token))
                    part = jnp.where(allowed, part, NEGATIVE)
                scores.append(part)
            highest = scores[0]
            for part in scores[1:]:
                highest = jnp.maximum(highest, part)
            highest = jnp.max(highest, axis=1, keepdims=True)
            weights = [
                jnp.exp2((part - highest) * LOG2_SCALE).astype(jnp.bfloat16) for part in scores
            ]
            weights = jnp.concatenate(weights, axis=1) if chunks > 1 else weights[0]
            attended = jnp.dot(
                weights, values[: chunks * width, :], preferred_element_type=jnp.float32
            )
            result = (attended[:, :HD] / attended[:, HD:]).astype(jnp.bfloat16)
            for r in range(PER):
                out_ref[rows, r * HD : (r + 1) * HD] = result[r * BLOCK : (r + 1) * BLOCK, :]

        for chunks in range(1, CAPACITY // CHUNK + 1):
            pl.when((filled + CHUNK - 1) // CHUNK == chunks)(lambda chunks=chunks: run(chunks))


def local(query, key, value, vertical_blocks, slash_offsets, block_counts):
    device = lax.axis_index(AXES)
    place = jnp.stack([lax.axis_index(("c", "x", "y")), device]).astype(jnp.int32)
    bf16 = jnp.bfloat16
    packed = pl.pallas_call(
        pack_kernel,
        out_shape=jax.ShapeDtypeStruct((32, 32, HD), bf16),
        in_specs=[VMEM, VMEM],
        out_specs=VMEM,
    )(key, value)

    def shifted(array, distance):
        route = [(i, i + distance) for i in range(DEVICES - distance)]
        return lax.ppermute(array, AXES, route)

    second = shifted(packed, 2)
    fourth = shifted(packed, 4)

    spread = lax.all_to_all(packed, ("c", "x", "y"), 0, 0, tiled=True)
    owned = pl.pallas_call(
        pick_owned_kernel,
        out_shape=jax.ShapeDtypeStruct((8, MAXV, 16, HD), bf16),
        in_specs=[SMEM, SMEM, VMEM],
        out_specs=VMEM,
    )(place, vertical_blocks, spread.reshape(32, 2, 16, HD))
    layers = lax.all_to_all(owned, ("zh", "zl"), 0, 0, tiled=True)
    pieces = pl.pallas_call(
        pick_layer_kernel,
        out_shape=jax.ShapeDtypeStruct((16, MAXV, 16, HD), bf16),
        in_specs=[SMEM, SMEM, VMEM],
        out_specs=VMEM,
    )(place, vertical_blocks, layers)
    near = lax.all_to_all(pieces, ("x", "y"), 0, 0, tiled=True)
    far = lax.ppermute(near, "c", [(0, 1), (1, 0)])

    odd = shifted(jnp.stack([packed, second]), 1)

    slab_shape = (KVH, 2, 4, 2, 16, HD)
    pair_shape = (2, 2, 4, MAXV, 16, HD)
    columns = pl.BlockSpec(
        (2 * BLOCK, PER * HD),
        lambda i, place_ref, *_: (0, (((place_ref[0] >> 4) ^ (i >> 1)) << 1) | (i & 1)),
    )
    return pl.pallas_call(
        attend_kernel,
        out_shape=jax.ShapeDtypeStruct((2 * BLOCK, QH * HD), bf16),
        grid_spec=pltpu.PrefetchScalarGridSpec(
            num_scalar_prefetch=4,
            grid=(KVH,),
            in_specs=[columns] + [ANY] * 6,
            out_specs=columns,
            scratch_shapes=[
                pltpu.VMEM((5,) + slab_shape, bf16),
                pltpu.VMEM((2,) + pair_shape, bf16),
                pltpu.VMEM((CAPACITY * BLOCK, HD), bf16),
                pltpu.VMEM((CAPACITY * BLOCK, 2 * HD), bf16),
                pltpu.SemaphoreType.DMA((7,)),
            ],
        ),
        compiler_params=pltpu.CompilerParams(vmem_limit_bytes=40 * 1024 * 1024),
        cost_estimate=pl.CostEstimate(
            flops=2_000_000_000, bytes_accessed=4_000_000, transcendentals=4_000_000
        ),
    )(
        place,
        vertical_blocks,
        slash_offsets,
        block_counts,
        query,
        packed.reshape(slab_shape),
        second.reshape(slab_shape),
        fourth.reshape(slab_shape),
        odd.reshape((2,) + slab_shape),
        near.reshape(pair_shape),
        far.reshape(pair_shape),
    )


def solution(mesh):
    finer = Mesh(np.asarray(mesh.devices).reshape(SIZES), AXES)
    return jax.shard_map(
        local,
        mesh=finer,
        in_specs=(P(AXES), P(AXES), P(AXES), P(), P(), P()),
        out_specs=P(AXES),
        check_vma=False,
    )
```

```python
import math
import jax
import jax.numpy as jnp
import numpy as np
from jax import lax
from jax.experimental import pallas as pl
from jax.experimental.pallas import tpu as pltpu
from jax.sharding import Mesh, PartitionSpec as P

QH = 28
KVH = 4
HD = 128
BLOCK = 64
MAXV = 8
MAXS = 9
PER = QH // KVH
SIZES = (2, 2, 4, 4, 4)
AXES = ("zh", "c", "x", "y", "zl")
DEVICES = 256
CHUNK = 4
CAPACITY = 5 * CHUNK
NEGATIVE = -1e30
LOG2_SCALE = math.log2(math.e) * HD ** (-0.5)
VMEM = pl.BlockSpec(memory_space=pltpu.VMEM)
SMEM = pl.BlockSpec(memory_space=pltpu.SMEM)
ANY = pl.BlockSpec(memory_space=pl.ANY)
THREE_BACK = [(0, 3), (1, 0), (2, 1), (3, 2)]


def owner_plane(block):
    return (block >> 3) & 31


def owner_layer(block):
    return ((block >> 8) << 2) | ((block >> 1) & 3)


def pack_kernel(key_ref, value_ref, packed_ref, slab_ref):
    for h in range(KVH):
        for kv, source in enumerate((key_ref, value_ref)):
            for block in range(2):
                tokens = source[block * BLOCK : (block + 1) * BLOCK, h * HD : (h + 1) * HD]
                slab_ref[h, kv, block] = tokens
                for quarter in range(4):
                    packed_ref[h * 8 + kv * 4 + quarter, block * 16 : block * 16 + 16, :] = tokens[
                        quarter * 16 : quarter * 16 + 16
                    ]


def pick_owned_kernel(
    place_ref, vertical_ref, received_ref, own_ref, fourth_ref, first_ref, out_ref, chosen_ref
):
    head = place_ref[0] >> 3
    for j in range(MAXV):
        block = vertical_ref[head, j]
        piece = received_ref[owner_plane(block), block & 1]
        for copy in range(8):
            out_ref[copy, j] = piece
    first_of_line = (place_ref[1] & 3) == 0

    @pl.when(first_of_line)
    def _():
        chosen_ref[...] = own_ref[...]

    @pl.when(jnp.logical_not(first_of_line))
    def _():
        chosen_ref[...] = fourth_ref[...]


def pick_layer_kernel(place_ref, vertical_ref, received_ref, chosen_ref, first_ref, *refs):
    out_ref = refs[-3]
    head = place_ref[0] >> 3
    for j in range(MAXV):
        piece = received_ref[owner_layer(vertical_ref[head, j]), j]
        for copy in range(16):
            out_ref[copy, j] = piece


def attend_kernel(
    place_ref,
    vertical_ref,
    offsets_ref,
    counts_ref,
    query_ref,
    own_ref,
    fourth_ref,
    third_ref,
    second_ref,
    first_ref,
    near_ref,
    far_ref,
    out_ref,
    slab,
    pairs,
    keys,
    values,
    sems,
):
    head = pl.program_id(0)
    device = place_ref[1]

    @pl.when(head == 0)
    def _():
        mine = (place_ref[0] >> 4) * 2
        copies = [
            pltpu.make_async_copy(fourth_ref, slab.at[0], sems.at[0]),
            pltpu.make_async_copy(third_ref, slab.at[1], sems.at[1]),
            pltpu.make_async_copy(second_ref, slab.at[2], sems.at[2]),
            pltpu.make_async_copy(first_ref, slab.at[3], sems.at[3]),
            pltpu.make_async_copy(own_ref, slab.at[4], sems.at[4]),
            pltpu.make_async_copy(near_ref, pairs.at[pl.ds(mine, 2)], sems.at[5]),
            pltpu.make_async_copy(far_ref, pairs.at[pl.ds(2 - mine, 2)], sems.at[6]),
        ]
        for copy in copies:
            copy.start()
        keys[...] = jnp.zeros_like(keys)
        values[:, :HD] = jnp.zeros((CAPACITY * BLOCK, HD), jnp.bfloat16)
        values[:, HD:] = jnp.ones((CAPACITY * BLOCK, HD), jnp.bfloat16)
        for copy in copies:
            copy.wait()

    def put(slot, key, value):
        rows = pl.ds(pl.multiple_of(slot * BLOCK, BLOCK), BLOCK)
        keys[rows, :] = key.reshape(BLOCK, HD)
        values[rows, :HD] = value.reshape(BLOCK, HD)

    for local_block in range(2):
        block = device * 2 + local_block
        put(0, slab[4, head, 0, local_block], slab[4, head, 1, local_block])
        filled = jnp.int32(1)
        near = jnp.int32(0)
        for j in range(MAXV):
            vertical = vertical_ref[head, j]
            put(filled, pairs[head, 0, :, j], pairs[head, 1, :, j])
            live = (j < counts_ref[head, 0]) & (vertical < block)
            distance = block - vertical
            near = jnp.where(live & (distance <= 8), near | (1 << jnp.clip(distance, 0, 8)), near)
            filled = jnp.where(live, filled + 1, filled)
        for i in range(1, MAXS):
            offset = offsets_ref[head, i]
            live = (
                (i < counts_ref[head, 1]) & (block >= offset) & (((near >> offset) & 1) == 0)
            )
            place = local_block + 8 - offset
            put(
                filled,
                slab[place >> 1, head, 0, place & 1],
                slab[place >> 1, head, 1, place & 1],
            )
            filled = jnp.where(live, filled + 1, filled)

        rows = slice(local_block * BLOCK, (local_block + 1) * BLOCK)
        queries = jnp.concatenate(
            [query_ref[rows, r * HD : (r + 1) * HD] for r in range(PER)], axis=0
        )

        def run(chunks):
            width = CHUNK * BLOCK
            total = PER * BLOCK
            scores = []
            for chunk in range(chunks):
                part = lax.dot_general(
                    queries,
                    keys[chunk * width : (chunk + 1) * width, :],
                    (((1,), (1,)), ((), ())),
                    preferred_element_type=jnp.float32,
                )
                if chunk == 0 or chunk == chunks - 1:
                    lane = lax.broadcasted_iota(jnp.int32, (total, width), 1)
                    allowed = lane + chunk * width < filled * BLOCK
                    if chunk == 0:
                        token = lax.broadcasted_iota(jnp.int32, (total, width), 0) % BLOCK
                        allowed = allowed & ((lane >= BLOCK) | (lane <= token))
                    part = jnp.where(allowed, part, NEGATIVE)
                scores.append(part)
            highest = scores[0]
            for part in scores[1:]:
                highest = jnp.maximum(highest, part)
            highest = jnp.max(highest, axis=1, keepdims=True)
            weights = [
                jnp.exp2((part - highest) * LOG2_SCALE).astype(jnp.bfloat16) for part in scores
            ]
            weights = jnp.concatenate(weights, axis=1) if chunks > 1 else weights[0]
            attended = jnp.dot(
                weights, values[: chunks * width, :], preferred_element_type=jnp.float32
            )
            result = (attended[:, :HD] / attended[:, HD:]).astype(jnp.bfloat16)
            for r in range(PER):
                out_ref[rows, r * HD : (r + 1) * HD] = result[r * BLOCK : (r + 1) * BLOCK, :]

        for chunks in range(1, CAPACITY // CHUNK + 1):
            pl.when((filled + CHUNK - 1) // CHUNK == chunks)(lambda chunks=chunks: run(chunks))


def hand_on_kernel(*refs):
    pass


def hold(*arrays):
    count = len(arrays)
    return pl.pallas_call(
        hand_on_kernel,
        out_shape=tuple(jax.ShapeDtypeStruct(array.shape, array.dtype) for array in arrays),
        in_specs=[ANY] * count,
        out_specs=(ANY,) * count,
        input_output_aliases={i: i for i in range(count)},
        cost_estimate=pl.CostEstimate(
            flops=40_000_000_000, bytes_accessed=1_000_000, transcendentals=0
        ),
    )(*arrays)


def after(array, *others):
    return pl.pallas_call(
        hand_on_kernel,
        out_shape=jax.ShapeDtypeStruct(array.shape, array.dtype),
        in_specs=[ANY] * (1 + len(others)),
        out_specs=ANY,
        input_output_aliases={0: 0},
    )(array, *others)


def local(query, key, value, vertical_blocks, slash_offsets, block_counts):
    device = lax.axis_index(AXES)
    place = jnp.stack([lax.axis_index(("c", "x", "y")), device, lax.axis_index(("zh", "zl"))]).astype(jnp.int32)
    bf16 = jnp.bfloat16
    slab_shape = jax.ShapeDtypeStruct((KVH, 2, 2, BLOCK, HD), bf16)
    packed, own = pl.pallas_call(
        pack_kernel,
        out_shape=(jax.ShapeDtypeStruct((32, 32, HD), bf16), slab_shape),
        in_specs=[VMEM, VMEM],
        out_specs=(VMEM, VMEM),
    )(key, value)

    def shifted(array, distance):
        route = [(i, i + distance) for i in range(DEVICES - distance)]
        return lax.ppermute(array, AXES, route)

    fourth = shifted(own, 4)
    first = shifted(own, 1)
    spread = lax.all_to_all(packed, ("c", "x", "y"), 0, 0, tiled=True)
    owned, chosen = pl.pallas_call(
        pick_owned_kernel,
        out_shape=(jax.ShapeDtypeStruct((8, MAXV, 16, HD), bf16), slab_shape),
        in_specs=[SMEM, SMEM, VMEM, VMEM, VMEM, VMEM],
        out_specs=(VMEM, VMEM),
    )(place, vertical_blocks, spread.reshape(32, 2, 16, HD), own, fourth, first)
    layers = lax.all_to_all(owned, ("zh", "zl"), 0, 0, tiled=True)
    late = [
    ]
    pieces, chosen, first = pl.pallas_call(
        pick_layer_kernel,
        out_shape=(jax.ShapeDtypeStruct((16, MAXV, 16, HD), bf16), slab_shape, slab_shape),
        in_specs=[SMEM, SMEM, VMEM, ANY, ANY] + [ANY] * len(late),
        out_specs=(VMEM, ANY, ANY),
        input_output_aliases={3: 1, 4: 2},
    )(place, vertical_blocks, layers, chosen, first, *late)
    third = lax.ppermute(chosen, "zl", THREE_BACK)
    second = shifted(first, 1)
    near = lax.all_to_all(pieces, ("x", "y"), 0, 0, tiled=True)
    third, second = hold(third, second)
    near = after(near, third, second)
    far = lax.ppermute(near, "c", [(0, 1), (1, 0)])

    pair_shape = (KVH, 2, 4, MAXV, 16, HD)
    half_shape = (KVH // 2, 2, 4, MAXV, 16, HD)
    columns = pl.BlockSpec(
        (2 * BLOCK, PER * HD),
        lambda i, *_: (0, i),
    )
    return pl.pallas_call(
        attend_kernel,
        out_shape=jax.ShapeDtypeStruct((2 * BLOCK, QH * HD), bf16),
        grid_spec=pltpu.PrefetchScalarGridSpec(
            num_scalar_prefetch=4,
            grid=(KVH,),
            in_specs=[columns] + [ANY] * 7,
            out_specs=columns,
            scratch_shapes=[
                pltpu.VMEM((5,) + slab_shape.shape, bf16),
                pltpu.VMEM(pair_shape, bf16),
                pltpu.VMEM((CAPACITY * BLOCK, HD), bf16),
                pltpu.VMEM((CAPACITY * BLOCK, 2 * HD), bf16),
                pltpu.SemaphoreType.DMA((7,)),
            ],
        ),
        compiler_params=pltpu.CompilerParams(vmem_limit_bytes=40 * 1024 * 1024),
        cost_estimate=pl.CostEstimate(
            flops=2_000_000_000, bytes_accessed=4_000_000, transcendentals=4_000_000
        ),
    )(
        place,
        vertical_blocks,
        slash_offsets,
        block_counts,
        query,
        own,
        fourth,
        third,
        second,
        first,
        near.reshape(half_shape),
        far.reshape(half_shape),
    )


def solution(mesh):
    finer = Mesh(np.asarray(mesh.devices).reshape(SIZES), AXES)
    return jax.shard_map(
        local,
        mesh=finer,
        in_specs=(P(AXES), P(AXES), P(AXES), P(), P(), P()),
        out_specs=P(AXES),
        check_vma=False,
    )
```

```python
import math
import jax
import jax.numpy as jnp
import numpy as np
from jax import lax
from jax.experimental import pallas as pl
from jax.experimental.pallas import tpu as pltpu
from jax.sharding import Mesh, PartitionSpec as P

QH = 28
KVH = 4
HD = 128
BLOCK = 64
MAXV = 8
MAXS = 9
PER = QH // KVH
SIZES = (2, 2, 4, 4, 4)
AXES = ("zh", "c", "x", "y", "zl")
DEVICES = 256
CHUNK = 2
CAPACITY = 9 * CHUNK
NEGATIVE = -1e30
LOG2_SCALE = math.log2(math.e) * HD ** (-0.5)
VMEM = pl.BlockSpec(memory_space=pltpu.VMEM)
SMEM = pl.BlockSpec(memory_space=pltpu.SMEM)
ANY = pl.BlockSpec(memory_space=pl.ANY)


def owner_plane(block):
    return (block >> 3) & 31


def owner_layer(block):
    return ((block >> 8) << 2) | ((block >> 1) & 3)


def pack_kernel(key_ref, value_ref, packed_ref, slab_ref):
    for h in range(KVH):
        for kv, source in enumerate((key_ref, value_ref)):
            for block in range(2):
                tokens = source[block * BLOCK : (block + 1) * BLOCK, h * HD : (h + 1) * HD]
                slab_ref[h, kv, block] = tokens
                for quarter in range(4):
                    packed_ref[h * 8 + kv * 4 + quarter, block * 16 : block * 16 + 16, :] = tokens[
                        quarter * 16 : quarter * 16 + 16
                    ]


def pick_owned_kernel(
    place_ref, vertical_ref, received_ref, first_ref, fourth_ref, out_ref
):
    head = place_ref[0] >> 3
    for j in range(MAXV):
        block = vertical_ref[head, j]
        piece = received_ref[owner_plane(block), block & 1]
        for copy in range(8):
            out_ref[copy, j] = piece


def pick_layer_kernel(place_ref, vertical_ref, received_ref, fourth_ref, first_ref, *refs):
    out_ref = refs[-3]
    head = place_ref[0] >> 3
    for j in range(MAXV):
        piece = received_ref[owner_layer(vertical_ref[head, j]), j]
        for copy in range(16):
            out_ref[copy, j] = piece


def attend_kernel(
    place_ref,
    vertical_ref,
    offsets_ref,
    counts_ref,
    query_ref,
    own_ref,
    fourth_ref,
    third_ref,
    second_ref,
    first_ref,
    near_ref,
    far_ref,
    out_ref,
    slab,
    pairs,
    keys,
    values,
    sems,
):
    head = pl.program_id(0)
    device = place_ref[1]

    @pl.when(head == 0)
    def _():
        mine = (place_ref[0] >> 4) * 2
        copies = [
            pltpu.make_async_copy(fourth_ref, slab.at[0], sems.at[0]),
            pltpu.make_async_copy(third_ref, slab.at[1], sems.at[1]),
            pltpu.make_async_copy(second_ref, slab.at[2], sems.at[2]),
            pltpu.make_async_copy(first_ref, slab.at[3], sems.at[3]),
            pltpu.make_async_copy(own_ref, slab.at[4], sems.at[4]),
            pltpu.make_async_copy(near_ref, pairs.at[pl.ds(mine, 2)], sems.at[5]),
            pltpu.make_async_copy(far_ref, pairs.at[pl.ds(2 - mine, 2)], sems.at[6]),
        ]
        for copy in copies:
            copy.start()
        keys[...] = jnp.zeros_like(keys)
        values[:, :HD] = jnp.zeros((CAPACITY * BLOCK, HD), jnp.bfloat16)
        values[:, HD:] = jnp.ones((CAPACITY * BLOCK, HD), jnp.bfloat16)
        for copy in copies:
            copy.wait()

    def put(slot, key, value):
        rows = pl.ds(pl.multiple_of(slot * BLOCK, BLOCK), BLOCK)
        keys[rows, :] = key.reshape(BLOCK, HD)
        values[rows, :HD] = value.reshape(BLOCK, HD)

    for local_block in range(2):
        block = device * 2 + local_block
        put(0, slab[4, head, 0, local_block], slab[4, head, 1, local_block])
        filled = jnp.int32(1)
        near = jnp.int32(0)
        for j in range(MAXV):
            vertical = vertical_ref[head, j]
            put(filled, pairs[head, 0, :, j], pairs[head, 1, :, j])
            live = (j < counts_ref[head, 0]) & (vertical < block)
            distance = block - vertical
            near = jnp.where(live & (distance <= 8), near | (1 << jnp.clip(distance, 0, 8)), near)
            filled = jnp.where(live, filled + 1, filled)
        for i in range(1, MAXS):
            offset = offsets_ref[head, i]
            live = (
                (i < counts_ref[head, 1]) & (block >= offset) & (((near >> offset) & 1) == 0)
            )
            place = local_block + 8 - offset
            put(
                filled,
                slab[place >> 1, head, 0, place & 1],
                slab[place >> 1, head, 1, place & 1],
            )
            filled = jnp.where(live, filled + 1, filled)

        rows = slice(local_block * BLOCK, (local_block + 1) * BLOCK)
        queries = jnp.concatenate(
            [query_ref[rows, r * HD : (r + 1) * HD] for r in range(PER)], axis=0
        )

        def run(chunks):
            width = CHUNK * BLOCK
            total = PER * BLOCK
            scores = []
            for chunk in range(chunks):
                part = lax.dot_general(
                    queries,
                    keys[chunk * width : (chunk + 1) * width, :],
                    (((1,), (1,)), ((), ())),
                    preferred_element_type=jnp.float32,
                )
                if chunk == 0 or chunk == chunks - 1:
                    lane = lax.broadcasted_iota(jnp.int32, (total, width), 1)
                    allowed = lane + chunk * width < filled * BLOCK
                    if chunk == 0:
                        token = lax.broadcasted_iota(jnp.int32, (total, width), 0) % BLOCK
                        allowed = allowed & ((lane >= BLOCK) | (lane <= token))
                    part = jnp.where(allowed, part, NEGATIVE)
                scores.append(part)
            highest = scores[0]
            for part in scores[1:]:
                highest = jnp.maximum(highest, part)
            highest = jnp.max(highest, axis=1, keepdims=True)
            weights = [
                jnp.exp2((part - highest) * LOG2_SCALE).astype(jnp.bfloat16) for part in scores
            ]
            weights = jnp.concatenate(weights, axis=1) if chunks > 1 else weights[0]
            attended = jnp.dot(
                weights, values[: chunks * width, :], preferred_element_type=jnp.float32
            )
            result = (attended[:, :HD] / attended[:, HD:]).astype(jnp.bfloat16)
            for r in range(PER):
                out_ref[rows, r * HD : (r + 1) * HD] = result[r * BLOCK : (r + 1) * BLOCK, :]

        for chunks in range(1, CAPACITY // CHUNK + 1):
            pl.when((filled + CHUNK - 1) // CHUNK == chunks)(lambda chunks=chunks: run(chunks))


def hand_on_kernel(*refs):
    pass


def hold(*arrays):
    count = len(arrays)
    return pl.pallas_call(
        hand_on_kernel,
        out_shape=tuple(jax.ShapeDtypeStruct(array.shape, array.dtype) for array in arrays),
        in_specs=[ANY] * count,
        out_specs=(ANY,) * count,
        input_output_aliases={i: i for i in range(count)},
        cost_estimate=pl.CostEstimate(
            flops=40_000_000_000, bytes_accessed=1_000_000, transcendentals=0
        ),
    )(*arrays)


def after(array, *others):
    return pl.pallas_call(
        hand_on_kernel,
        out_shape=jax.ShapeDtypeStruct(array.shape, array.dtype),
        in_specs=[ANY] * (1 + len(others)),
        out_specs=ANY,
        input_output_aliases={0: 0},
    )(array, *others)


def local(query, key, value, vertical_blocks, slash_offsets, block_counts):
    device = lax.axis_index(AXES)
    place = jnp.stack([lax.axis_index(("c", "x", "y")), device, lax.axis_index(("zh", "zl"))]).astype(jnp.int32)
    bf16 = jnp.bfloat16
    slab_shape = jax.ShapeDtypeStruct((KVH, 2, 2, BLOCK, HD), bf16)
    packed, own = pl.pallas_call(
        pack_kernel,
        out_shape=(jax.ShapeDtypeStruct((32, 32, HD), bf16), slab_shape),
        in_specs=[VMEM, VMEM],
        out_specs=(VMEM, VMEM),
    )(key, value)

    def shifted(array, distance):
        route = [(i, (i + distance) % DEVICES) for i in range(DEVICES)]
        return lax.ppermute(array, AXES, route)

    fourth = shifted(own, 4)
    first = shifted(own, 1)
    spread = lax.all_to_all(packed, ("c", "x", "y"), 0, 0, tiled=True)
    owned = pl.pallas_call(
        pick_owned_kernel,
        out_shape=jax.ShapeDtypeStruct((8, MAXV, 16, HD), bf16),
        in_specs=[SMEM, SMEM, VMEM, VMEM, VMEM],
        out_specs=VMEM,
    )(place, vertical_blocks, spread.reshape(32, 2, 16, HD), first, fourth)
    layers = lax.all_to_all(owned, ("zh", "zl"), 0, 0, tiled=True)
    late = [
    ]
    pieces, fourth, first = pl.pallas_call(
        pick_layer_kernel,
        out_shape=(jax.ShapeDtypeStruct((16, MAXV, 16, HD), bf16), slab_shape, slab_shape),
        in_specs=[SMEM, SMEM, VMEM, ANY, ANY] + [ANY] * len(late),
        out_specs=(VMEM, ANY, ANY),
        input_output_aliases={3: 1, 4: 2},
    )(place, vertical_blocks, layers, fourth, first, *late)
    third = shifted(fourth, -1)
    second = shifted(first, 1)
    near = lax.all_to_all(pieces, ("x", "y"), 0, 0, tiled=True)
    third, second = hold(third, second)
    near = after(near, third, second)
    far = lax.ppermute(near, "c", [(0, 1), (1, 0)])

    pair_shape = (KVH, 2, 4, MAXV, 16, HD)
    half_shape = (KVH // 2, 2, 4, MAXV, 16, HD)
    columns = pl.BlockSpec(
        (2 * BLOCK, PER * HD),
        lambda i, *_: (0, i),
    )
    return pl.pallas_call(
        attend_kernel,
        out_shape=jax.ShapeDtypeStruct((2 * BLOCK, QH * HD), bf16),
        grid_spec=pltpu.PrefetchScalarGridSpec(
            num_scalar_prefetch=4,
            grid=(KVH,),
            in_specs=[columns] + [ANY] * 7,
            out_specs=columns,
            scratch_shapes=[
                pltpu.VMEM((5,) + slab_shape.shape, bf16),
                pltpu.VMEM(pair_shape, bf16),
                pltpu.VMEM((CAPACITY * BLOCK, HD), bf16),
                pltpu.VMEM((CAPACITY * BLOCK, 2 * HD), bf16),
                pltpu.SemaphoreType.DMA((7,)),
            ],
        ),
        compiler_params=pltpu.CompilerParams(vmem_limit_bytes=40 * 1024 * 1024),
        cost_estimate=pl.CostEstimate(
            flops=2_000_000_000, bytes_accessed=4_000_000, transcendentals=4_000_000
        ),
    )(
        place,
        vertical_blocks,
        slash_offsets,
        block_counts,
        query,
        own,
        fourth,
        third,
        second,
        first,
        near.reshape(half_shape),
        far.reshape(half_shape),
    )


def solution(mesh):
    finer = Mesh(np.asarray(mesh.devices).reshape(SIZES), AXES)
    return jax.shard_map(
        local,
        mesh=finer,
        in_specs=(P(AXES), P(AXES), P(AXES), P(), P(), P()),
        out_specs=P(AXES),
        check_vma=False,
    )
```

```python
import math
import jax
import jax.numpy as jnp
import numpy as np
from jax import lax
from jax.experimental import pallas as pl
from jax.experimental.pallas import tpu as pltpu
from jax.sharding import Mesh, PartitionSpec as P

QH = 28
KVH = 4
HD = 128
BLOCK = 64
MAXV = 8
MAXS = 9
PER = QH // KVH
SIZES = (2, 2, 4, 4, 4)
AXES = ("zh", "c", "x", "y", "zl")
DEVICES = 256
CHUNK = 2
CAPACITY = 9 * CHUNK
NEGATIVE = -1e30
LOG2_SCALE = math.log2(math.e) * HD ** (-0.5)
VMEM = pl.BlockSpec(memory_space=pltpu.VMEM)
SMEM = pl.BlockSpec(memory_space=pltpu.SMEM)
ANY = pl.BlockSpec(memory_space=pl.ANY)


def owner_plane(block):
    return (block >> 3) & 31


def owner_layer(block):
    return ((block >> 8) << 2) | ((block >> 1) & 3)


def pack_kernel(key_ref, value_ref, packed_ref, slab_ref):
    for h in range(KVH):
        for kv, source in enumerate((key_ref, value_ref)):
            for block in range(2):
                tokens = source[block * BLOCK : (block + 1) * BLOCK, h * HD : (h + 1) * HD]
                slab_ref[h, kv, block] = tokens
                for quarter in range(4):
                    packed_ref[h * 8 + kv * 4 + quarter, block * 16 : block * 16 + 16, :] = tokens[
                        quarter * 16 : quarter * 16 + 16
                    ]


def pick_owned_kernel(
    place_ref, vertical_ref, received_ref, first_ref, fourth_ref, out_ref
):
    head = place_ref[0] >> 3
    for j in range(MAXV):
        block = vertical_ref[head, j]
        piece = received_ref[owner_plane(block), block & 1]
        for copy in range(8):
            out_ref[copy, j] = piece


def pick_layer_kernel(place_ref, vertical_ref, received_ref, fourth_ref, first_ref, *refs):
    out_ref = refs[-3]
    head = place_ref[0] >> 3
    for j in range(MAXV):
        piece = received_ref[owner_layer(vertical_ref[head, j]), j]
        for copy in range(16):
            out_ref[copy, j] = piece


def attend_kernel(
    place_ref,
    vertical_ref,
    offsets_ref,
    counts_ref,
    query_ref,
    own_ref,
    fourth_ref,
    third_ref,
    second_ref,
    first_ref,
    near_ref,
    far_ref,
    out_ref,
    slab,
    pairs,
    keys,
    values,
    sems,
):
    head = pl.program_id(0)
    device = place_ref[1]

    @pl.when(head == 0)
    def _():
        mine = (place_ref[0] >> 4) * 2
        copies = [
            pltpu.make_async_copy(fourth_ref, slab.at[0], sems.at[0]),
            pltpu.make_async_copy(third_ref, slab.at[1], sems.at[1]),
            pltpu.make_async_copy(second_ref, slab.at[2], sems.at[2]),
            pltpu.make_async_copy(first_ref, slab.at[3], sems.at[3]),
            pltpu.make_async_copy(own_ref, slab.at[4], sems.at[4]),
            pltpu.make_async_copy(near_ref, pairs.at[pl.ds(mine, 2)], sems.at[5]),
            pltpu.make_async_copy(far_ref, pairs.at[pl.ds(2 - mine, 2)], sems.at[6]),
        ]
        for copy in copies:
            copy.start()
        keys[...] = jnp.zeros_like(keys)
        values[:, :HD] = jnp.zeros((CAPACITY * BLOCK, HD), jnp.bfloat16)
        values[:, HD:] = jnp.ones((CAPACITY * BLOCK, HD), jnp.bfloat16)
        for copy in copies:
            copy.wait()

    def put(slot, key, value):
        rows = pl.ds(pl.multiple_of(slot * BLOCK, BLOCK), BLOCK)
        keys[rows, :] = key.reshape(BLOCK, HD)
        values[rows, :HD] = value.reshape(BLOCK, HD)

    for local_block in range(2):
        block = device * 2 + local_block
        put(0, slab[4, head, 0, local_block], slab[4, head, 1, local_block])
        filled = jnp.int32(1)
        near = jnp.int32(0)
        for j in range(MAXV):
            vertical = vertical_ref[head, j]
            put(filled, pairs[head, 0, :, j], pairs[head, 1, :, j])
            live = (j < counts_ref[head, 0]) & (vertical < block)
            distance = block - vertical
            near = jnp.where(live & (distance <= 8), near | (1 << jnp.clip(distance, 0, 8)), near)
            filled = jnp.where(live, filled + 1, filled)
        for i in range(1, MAXS):
            offset = offsets_ref[head, i]
            live = (
                (i < counts_ref[head, 1]) & (block >= offset) & (((near >> offset) & 1) == 0)
            )
            place = local_block + 8 - offset
            put(
                filled,
                slab[place >> 1, head, 0, place & 1],
                slab[place >> 1, head, 1, place & 1],
            )
            filled = jnp.where(live, filled + 1, filled)

        rows = slice(local_block * BLOCK, (local_block + 1) * BLOCK)
        queries = jnp.concatenate(
            [query_ref[rows, r * HD : (r + 1) * HD] for r in range(PER)], axis=0
        )

        def run(chunks):
            width = CHUNK * BLOCK
            total = PER * BLOCK
            scores = []
            for chunk in range(chunks):
                part = lax.dot_general(
                    queries,
                    keys[chunk * width : (chunk + 1) * width, :],
                    (((1,), (1,)), ((), ())),
                    preferred_element_type=jnp.float32,
                )
                if chunk == 0 or chunk == chunks - 1:
                    lane = lax.broadcasted_iota(jnp.int32, (total, width), 1)
                    allowed = lane + chunk * width < filled * BLOCK
                    if chunk == 0:
                        token = lax.broadcasted_iota(jnp.int32, (total, width), 0) % BLOCK
                        allowed = allowed & ((lane >= BLOCK) | (lane <= token))
                    part = jnp.where(allowed, part, NEGATIVE)
                scores.append(part)
            highest = scores[0]
            for part in scores[1:]:
                highest = jnp.maximum(highest, part)
            highest = jnp.max(highest, axis=1, keepdims=True)
            weights = [
                jnp.exp2((part - highest) * LOG2_SCALE).astype(jnp.bfloat16) for part in scores
            ]
            weights = jnp.concatenate(weights, axis=1) if chunks > 1 else weights[0]
            attended = jnp.dot(
                weights, values[: chunks * width, :], preferred_element_type=jnp.float32
            )
            result = (attended[:, :HD] / attended[:, HD:]).astype(jnp.bfloat16)
            for r in range(PER):
                out_ref[rows, r * HD : (r + 1) * HD] = result[r * BLOCK : (r + 1) * BLOCK, :]

        for chunks in range(1, CAPACITY // CHUNK + 1):
            pl.when((filled + CHUNK - 1) // CHUNK == chunks)(lambda chunks=chunks: run(chunks))


def hand_on_kernel(*refs):
    pass


def hold(*arrays):
    count = len(arrays)
    return pl.pallas_call(
        hand_on_kernel,
        out_shape=tuple(jax.ShapeDtypeStruct(array.shape, array.dtype) for array in arrays),
        in_specs=[ANY] * count,
        out_specs=(ANY,) * count,
        input_output_aliases={i: i for i in range(count)},
        cost_estimate=pl.CostEstimate(
            flops=40_000_000_000, bytes_accessed=1_000_000, transcendentals=0
        ),
    )(*arrays)


def after(array, *others):
    return pl.pallas_call(
        hand_on_kernel,
        out_shape=jax.ShapeDtypeStruct(array.shape, array.dtype),
        in_specs=[ANY] * (1 + len(others)),
        out_specs=ANY,
        input_output_aliases={0: 0},
        cost_estimate=pl.CostEstimate(
            flops=40_000_000_000, bytes_accessed=1_000_000, transcendentals=0
        ),
    )(array, *others)


def local(query, key, value, vertical_blocks, slash_offsets, block_counts):
    device = lax.axis_index(AXES)
    place = jnp.stack([lax.axis_index(("c", "x", "y")), device, lax.axis_index(("zh", "zl"))]).astype(jnp.int32)
    bf16 = jnp.bfloat16
    slab_shape = jax.ShapeDtypeStruct((KVH, 2, 2, BLOCK, HD), bf16)
    packed, own = pl.pallas_call(
        pack_kernel,
        out_shape=(jax.ShapeDtypeStruct((32, 32, HD), bf16), slab_shape),
        in_specs=[VMEM, VMEM],
        out_specs=(VMEM, VMEM),
    )(key, value)

    def shifted(array, distance):
        route = [(i, (i + distance) % DEVICES) for i in range(DEVICES)]
        return lax.ppermute(array, AXES, route)

    fourth = shifted(own, 4)
    first = shifted(own, 1)
    spread = lax.all_to_all(packed, ("c", "x", "y"), 0, 0, tiled=True)
    owned = pl.pallas_call(
        pick_owned_kernel,
        out_shape=jax.ShapeDtypeStruct((8, MAXV, 16, HD), bf16),
        in_specs=[SMEM, SMEM, VMEM, VMEM, VMEM],
        out_specs=VMEM,
    )(place, vertical_blocks, spread.reshape(32, 2, 16, HD), first, fourth)
    layers = lax.all_to_all(owned, ("zh", "zl"), 0, 0, tiled=True)
    late = [
    ]
    pieces, fourth, first = pl.pallas_call(
        pick_layer_kernel,
        out_shape=(jax.ShapeDtypeStruct((16, MAXV, 16, HD), bf16), slab_shape, slab_shape),
        in_specs=[SMEM, SMEM, VMEM, ANY, ANY] + [ANY] * len(late),
        out_specs=(VMEM, ANY, ANY),
        input_output_aliases={3: 1, 4: 2},
    )(place, vertical_blocks, layers, fourth, first, *late)
    third = shifted(fourth, -1)
    second = shifted(first, 1)
    near = lax.all_to_all(pieces, ("x", "y"), 0, 0, tiled=True)
    third, second = hold(third, second)
    place = after(place, third, second)
    far = lax.ppermute(near, "c", [(0, 1), (1, 0)])

    pair_shape = (KVH, 2, 4, MAXV, 16, HD)
    half_shape = (KVH // 2, 2, 4, MAXV, 16, HD)
    columns = pl.BlockSpec(
        (2 * BLOCK, PER * HD),
        lambda i, *_: (0, i),
    )
    return pl.pallas_call(
        attend_kernel,
        out_shape=jax.ShapeDtypeStruct((2 * BLOCK, QH * HD), bf16),
        grid_spec=pltpu.PrefetchScalarGridSpec(
            num_scalar_prefetch=4,
            grid=(KVH,),
            in_specs=[columns] + [ANY] * 7,
            out_specs=columns,
            scratch_shapes=[
                pltpu.VMEM((5,) + slab_shape.shape, bf16),
                pltpu.VMEM(pair_shape, bf16),
                pltpu.VMEM((CAPACITY * BLOCK, HD), bf16),
                pltpu.VMEM((CAPACITY * BLOCK, 2 * HD), bf16),
                pltpu.SemaphoreType.DMA((7,)),
            ],
        ),
        compiler_params=pltpu.CompilerParams(vmem_limit_bytes=40 * 1024 * 1024),
        cost_estimate=pl.CostEstimate(
            flops=2_000_000_000, bytes_accessed=4_000_000, transcendentals=4_000_000
        ),
    )(
        place,
        vertical_blocks,
        slash_offsets,
        block_counts,
        query,
        own,
        fourth,
        third,
        second,
        first,
        near.reshape(half_shape),
        far.reshape(half_shape),
    )


def solution(mesh):
    finer = Mesh(np.asarray(mesh.devices).reshape(SIZES), AXES)
    return jax.shard_map(
        local,
        mesh=finer,
        in_specs=(P(AXES), P(AXES), P(AXES), P(), P(), P()),
        out_specs=P(AXES),
        check_vma=False,
    )
```
